32 devices in a mesh: seq: 8 (over z, y), tp: 4 (over x, core).
Axes of the slice: x: 2, y: 2, z: 4, core: 2. Of those that a mesh axis runs over, the one named last changes fastest.
Arguments:
- db_tokens: int32 [4096, 128], P('seq'), may hold values from 0 to 16383
- db_parent: int32 [4096, 128], P('seq'), may hold values from 0 to 126, as said below
- db_depth: int32 [4096, 128], P('seq'), may hold values from 0 to 31, as said below
- nb_rows: int32 [64, 2], P('seq'), may hold values from 0 to 4095, as said below
- seq_start: int32 [64], P('seq'), may hold values 0 or 1
- table: bfloat16 [16384, 1024], P(None, 'tp'), may hold values from -40 to 40
- depth_table: bfloat16 [32, 1024], P(None, 'tp'), may hold values from -3 to 3
- enc_gain: float32 [1024], replicated, may hold values from 0.25 to 1.75
- enc_qkv: bfloat16 [1024, 3, 1024], P('seq', None, 'tp'), may hold values from -0.1875 to 0.1875
- tree_bias: float32 [8], replicated, may hold values from 1 to 4
- enc_wo: bfloat16 [1024, 1024], P('tp', 'seq'), may hold values from -0.1875 to 0.1875
- cond_kv: bfloat16 [4096, 2, 1024], P('seq', None, 'tp'), may hold values from -150 to 150
- queries: bfloat16 [4096, 4096], P('seq', 'tp'), may hold values from -150 to 150
- cca_kv: bfloat16 [1024, 2, 512], P('seq', None, 'tp'), may hold values from -0.1875 to 0.1875
Outputs:
- attended: bfloat16 [4096, 4096], P('seq', 'tp')
The draws below stay inside these ranges and needn't reach their ends.
Inputs may be any that keep to these rules, and one draw needn't show every extreme that they name: `db_parent`: position 0 of every stored neighbour is its own parent; every other position's parent is one of the three positions just before it. `db_depth`: position 0 has depth 0; every other position has its parent's depth plus one, capped at 31. `nb_rows`: rows 512 * i to 512 * (i + 1) - 1 of the database lie on index i of seq. Of the 16 neighbours of one index's blocks at most 4 lie on any one index; at most 32 neighbours of all blocks lie on one index, and in every draw some index holds exactly 32.
All inputs are finite; a program needn't handle non-finite values. No bound on the sum of `seq_start` on one device may be relied on, other than what follows from the above.
Results may differ from the reference program's by a relative error of at most 0.0223.
The reference program's roundings to bfloat16 on the way count: a program that leaves them out, or rounds other values in their place, can miss the bound.
Values may be sent and summed in bfloat16 or wider, within the bound.
A program may use at most 128 MiB of HBM per device.

```python
import math
import jax
import jax.numpy as jnp
import numpy as np
from jax import lax

E = 1024
EH = 8
HD = 128
HQ = 32
KVH = 4
VOCAB = 16384
CL = 64
NL = 128
KN = 2
DEPTHS = 32
CH_DEV = 8
DB_DEV = 512
BLOCKS = 64
TOKENS = 4096
DB_ROWS = 4096
N_SEQ = 8


def tree_layout(key):
    steps_back = jax.random.randint(key, (DB_ROWS, NL), 1, 4)
    positions = jnp.arange(NL, dtype=jnp.int32)[None, :]
    parents = jnp.maximum(positions - steps_back, 0).astype(jnp.int32)

    def advance(column, depths):
        parent_col = lax.dynamic_slice_in_dim(parents, column, 1, 1)
        parent_depth = jnp.take_along_axis(depths, parent_col, axis=1)
        updated = jnp.minimum(parent_depth + 1, DEPTHS - 1).astype(jnp.int32)
        return lax.dynamic_update_slice_in_dim(depths, updated, column, 1)
    depths = lax.fori_loop(1, NL, advance, jnp.zeros((DB_ROWS, NL), jnp.int32))
    return (parents, depths)


def draw_db_parent(key, part):
    parents, depths = tree_layout(jax.random.fold_in(key, 11))
    return parents


def draw_db_depth(key, part):
    parents, depths = tree_layout(jax.random.fold_in(key, 11))
    return depths


def draw_nb_rows(key, part):
    subkeys = jax.random.split(jax.random.fold_in(key, 51), 4)
    per_device = KN * CH_DEV
    holders = jax.random.permutation(subkeys[0], N_SEQ)
    offset = jax.random.randint(subkeys[1], (), 0, N_SEQ)
    ordering = jax.vmap(lambda subkey: jax.random.permutation(subkey, per_device))(jax.random.split(subkeys[2], N_SEQ))
    source = jnp.arange(N_SEQ, dtype=jnp.int32)[:, None]
    virtual = (source + offset + ordering) % N_SEQ
    midway = N_SEQ // 2
    quarter = N_SEQ // 4
    position = jnp.where(virtual < midway, virtual, jnp.where(virtual < midway + quarter, virtual - midway, virtual))
    holder = holders[position]
    stored_row = jax.random.randint(subkeys[3], (N_SEQ, per_device), 0, DB_DEV)
    return (holder * DB_DEV + stored_row).reshape(BLOCKS, KN).astype(jnp.int32)


def draw_table(key, part):
    subkeys = jax.random.split(jax.random.fold_in(key, 21), 3)
    column_scale = jnp.exp(jax.random.uniform(subkeys[1], (1, E), jnp.float32, jnp.log(0.3), jnp.log(3.0)))
    row_scale = jnp.exp(jax.random.uniform(subkeys[2], (VOCAB, 1), jnp.float32, jnp.log(0.5), jnp.log(2.0)))
    base = jnp.clip(jax.random.normal(subkeys[0], (VOCAB, E), jnp.float32), -6.0, 6.0)
    return (base * column_scale * row_scale).astype(jnp.bfloat16)


def draw_cond_kv(key, part):
    subkeys = jax.random.split(jax.random.fold_in(key, 41), 1)
    base = jnp.clip(jax.random.normal(subkeys[0], (TOKENS, 2, E), jnp.float32), -6.0, 6.0)
    return base.astype(jnp.bfloat16)


def draw_queries(key, part):
    subkeys = jax.random.split(jax.random.fold_in(key, 31), 1)
    base = jnp.clip(jax.random.normal(subkeys[0], (TOKENS, HQ * HD), jnp.float32), -6.0, 6.0)
    return base.astype(jnp.bfloat16)


def set_ends(entries, rng, smallest, high):
    index_at = [jax.random.randint(jax.random.fold_in(rng, axis), (), 0, length) for axis, length in enumerate(entries.shape)]
    widest = entries.shape.index(max(entries.shape))
    neighbour = index_at[:widest] + [(index_at[widest] + 1) % entries.shape[widest]] + index_at[widest + 1:]
    return entries.at[tuple(index_at)].set(smallest).at[tuple(neighbour)].set(high)


def levels(rng, shape, pieces, low, top_value):
    loudness = 1.0
    for dim, parts in pieces:
        draws = jax.random.uniform(jax.random.fold_in(jax.random.fold_in(rng, 6), dim), (parts,), jnp.float32, low / len(pieces), top_value / len(pieces))
        loudness = loudness * jnp.repeat(jnp.exp(draws), shape[dim] // parts).reshape((-1,) + (1,) * (len(shape) - 1 - dim))
    return loudness


def rank_table(amount, slope):
    portions = [(1 << 20) // math.isqrt(standing ** slope) + 1 for standing in range(1, amount + 1)]
    spread = 1 + sum(portions) // (1 << 30)
    return np.cumsum(np.array([max(1, weight // spread) for weight in portions]))


def skewed_ids(stream_key, extent, count, lean):
    grid = rank_table(count, lean)
    pick = jax.random.randint(jax.random.fold_in(stream_key, 1), extent, 0, int(grid[count - 1]))
    standing = jnp.searchsorted(jnp.asarray(grid, jnp.int32), pick, side="right")
    return jax.random.permutation(jax.random.fold_in(stream_key, 2), count)[standing].astype(jnp.int32)


def noise(rng, extent, width, limit, cuts=(), held_as=jnp.bfloat16):
    drawn = width * jax.random.normal(rng, extent, jnp.float32)
    if cuts:
        drawn = drawn * levels(rng, extent, cuts, -0.22, 0.18)
    return jnp.clip(drawn, -limit, limit).astype(held_as)


def setup_inputs(seed: int = 0) -> dict:
    key_list = jax.random.split(jax.random.key(seed), 15)
    db_tokens = set_ends(skewed_ids(key_list[0], (DB_ROWS, NL), VOCAB, 2), jax.random.fold_in(key_list[0], 3), 0, VOCAB - 1).astype(jnp.int32)
    db_parent = draw_db_parent(jax.random.fold_in(key_list[14], 71), 0)
    db_depth = draw_db_depth(jax.random.fold_in(key_list[14], 71), 0)
    nb_rows = draw_nb_rows(jax.random.fold_in(key_list[14], 71), 0)
    seq_start = set_ends((jax.random.randint(key_list[4], (BLOCKS,), 0, 8) < 1).astype(jnp.int32), jax.random.fold_in(key_list[4], 1), 0, 1)
    table = draw_table(jax.random.fold_in(key_list[14], 71), 0)
    depth_table = noise(key_list[6], (DEPTHS, E), 0.5, 3.0, ((1, 4),))
    enc_gain = jnp.clip(1.0 + 0.15 * jax.random.normal(key_list[7], (E,), jnp.float32), 0.25, 1.75)
    enc_qkv = noise(key_list[8], (E, 3, E), E ** -0.5, 0.1875, ((0, 8), (2, 4)))
    tree_bias = jnp.clip(jax.random.uniform(key_list[9], (EH,), jnp.float32, 1.0, 4.0), 1.0, 4.0)
    enc_wo = noise(key_list[10], (E, E), E ** -0.5, 0.1875, ((0, 4), (1, 8)))
    cond_kv = draw_cond_kv(jax.random.fold_in(key_list[14], 71), 0)
    queries = draw_queries(jax.random.fold_in(key_list[14], 71), 0)
    cca_kv = noise(key_list[13], (E, 2, KVH * HD), E ** -0.5, 0.1875, ((0, 8), (2, 4)))
    return dict(db_tokens=db_tokens, db_parent=db_parent, db_depth=db_depth, nb_rows=nb_rows, seq_start=seq_start, table=table, depth_table=depth_table, enc_gain=enc_gain, enc_qkv=enc_qkv, tree_bias=tree_bias, enc_wo=enc_wo, cond_kv=cond_kv, queries=queries, cca_kv=cca_kv)


def rounded(values):
    return lax.optimization_barrier(values.astype(jnp.bfloat16)).astype(jnp.float32)

def reference(db_tokens, db_parent, db_depth, nb_rows, seq_start, table, depth_table, enc_gain, enc_qkv, tree_bias, enc_wo, cond_kv, queries, cca_kv):
    score_scale = 1.0 / math.sqrt(HD)
    qkv_weight = enc_qkv.astype(jnp.float32)
    out_weight = enc_wo.astype(jnp.float32)
    kv_weight = cca_kv.astype(jnp.float32)
    conditioning = cond_kv.reshape(BLOCKS, CL, 2, E)
    query_heads = queries.reshape(BLOCKS, CL, HQ, HD)
    positions = jnp.arange(NL, dtype=jnp.int32)

    def encode(row_pair, cond_block):
        tokens = db_tokens[row_pair]
        parents = db_parent[row_pair]
        depths = db_depth[row_pair]
        embedded = (table[tokens].astype(jnp.float32) + depth_table[depths].astype(jnp.float32)).astype(jnp.bfloat16)
        embedded_f = embedded.astype(jnp.float32)
        normed = rounded(embedded_f * lax.rsqrt(lax.optimization_barrier(jnp.mean(embedded_f * embedded_f, axis=-1, keepdims=True)) + 1e-05) * enc_gain)
        projected = rounded(jnp.einsum('kne,eaf->knaf', normed, qkv_weight))
        query_enc = projected[:, :, 0].reshape(KN, NL, EH, HD)
        key_enc = projected[:, :, 1].reshape(KN, NL, EH, HD)
        value_enc = projected[:, :, 2].reshape(KN, NL, EH, HD)
        cond_keys = cond_block[:, 0].astype(jnp.float32).reshape(CL, EH, HD)
        cond_values = cond_block[:, 1].astype(jnp.float32).reshape(CL, EH, HD)
        self_scores = jnp.einsum('kihd,kjhd->khij', query_enc, key_enc) * score_scale
        parent_hit = (parents[:, :, None] == positions[None, None, :]).astype(jnp.float32)
        self_scores = self_scores + tree_bias[None, :, None, None] * parent_hit[:, None, :, :]
        cond_scores = jnp.einsum('kihd,rhd->khir', query_enc, cond_keys) * score_scale
        weights = rounded(jax.nn.softmax(jnp.concatenate([self_scores, cond_scores], axis=-1), axis=-1))
        mixed = jnp.einsum('khij,kjhd->kihd', weights[..., :NL], value_enc) + jnp.einsum('khir,rhd->kihd', weights[..., NL:], cond_values)
        mixed = rounded(mixed.reshape(KN, NL, EH * HD))
        encoded = rounded(embedded_f + jnp.einsum('knf,fe->kne', mixed, out_weight))
        keys_values = rounded(jnp.einsum('kne,eaf->knaf', encoded, kv_weight))
        return keys_values.reshape(KN * NL, 2, KVH, HD)

    def attend(query, keys_values):
        grouped = query.reshape(query.shape[0], KVH, HQ // KVH, HD)
        scores = jnp.einsum('tkgd,pkd->kgtp', grouped, keys_values[:, 0]) * score_scale
        weights = rounded(jax.nn.softmax(scores, axis=-1))
        output = jnp.einsum('kgtp,pkd->tkgd', weights, keys_values[:, 1])
        return output.astype(jnp.bfloat16).reshape(query.shape[0], HQ * HD)

    def advance(carried, inputs):
        row_pair, cond_block, query_block, start_flag, block_index = inputs
        current = encode(row_pair, cond_block)
        query_f = query_block.astype(jnp.float32)
        leading = attend(query_f[:CL - 1], carried)
        allowed = (block_index > 0) & (start_flag == 0)
        leading = jnp.where(allowed, leading, jnp.zeros_like(leading))
        trailing = attend(query_f[CL - 1:], current)
        return (current, jnp.concatenate([leading, trailing], axis=0))
    initial = jnp.zeros((KN * NL, 2, KVH, HD), jnp.float32)
    final_state, attended = lax.scan(advance, initial, (nb_rows, conditioning, query_heads, seq_start, jnp.arange(BLOCKS, dtype=jnp.int32)))
    return attended.reshape(TOKENS, HQ * HD)
```

```python
import functools
import math

import jax
import jax.numpy as jnp
from jax import lax
from jax.experimental import pallas as pl
from jax.experimental.pallas import tpu as pltpu
from jax.sharding import PartitionSpec as P

HD = 128
SCALE = 1.0 / math.sqrt(HD)
MESH = pl.DeviceIdType.MESH
PARTS = ((0, 3), (3, 2))
NT = (((1,), (1,)), ((), ()))


def enter(peers):
    barrier = pltpu.get_barrier_semaphore()
    for peer in peers:
        pl.semaphore_signal(barrier, inc=1, device_id=peer, device_id_type=MESH)
    pl.semaphore_wait(barrier, len(peers))


def gather_kernel(
    seq_size,
    tp_size,
    req_ref,
    tok_ref,
    dep_ref,
    par_ref,
    w_ref,
    cond_ref,
    full_ref,
    resp_ref,
    cond_out,
    asked,
    answer,
    w_send,
    w_recv,
    own_sem,
    q_send,
    q_recv,
    r_send,
    r_recv,
    c_send,
    c_recv,
):
    s, t = lax.axis_index("seq"), lax.axis_index("tp")
    deep = seq_size // 2
    rows = w_ref.shape[1]
    seq_peers = [(lax.rem(s + j, seq_size), t) for j in range(1, seq_size)]
    tp_peers = [(s, lax.rem(t + j, tp_size)) for j in range(1, tp_size)]
    enter(seq_peers + tp_peers)

    started = []
    requests = []
    for j in range(1, seq_size):
        peer = seq_peers[j - 1]
        copy = pltpu.make_async_remote_copy(
            req_ref.at[peer[0]], asked.at[s], q_send.at[j], q_recv.at[seq_size - j], peer, MESH
        )
        copy.start()
        requests.append(copy)

    a, b = s // 2, s % 2
    c, d = t // 2, t % 2

    def place(slot):
        k, fb, fc, fd = slot
        sa = lax.rem(a + k, deep)
        sb = 1 - b if fb else b
        sc = 1 - c if fc else c
        sd = 1 - d if fd else d
        return sa * 2 + sb, sc * 2 + sd

    def landing(part, slot):
        ps, pt = place(slot)
        first, count = PARTS[part]
        return full_ref.at[
            pt, pl.ds(first, count), pl.ds(pl.multiple_of(ps * rows, rows), rows), :
        ]

    def own(part):
        first, count = PARTS[part]
        return w_ref.at[pl.ds(first, count)]

    def send(part, slot, way, hop=0):
        k, fb, fc, fd = slot
        if way == "a":
            peer = (lax.rem(a + hop, deep) * 2 + b, t)
            index = ((deep - hop) % deep, fb, fc, fd)
        elif way == "b":
            peer = (a * 2 + 1 - b, t)
            index = (k, 1, fc, fd)
        elif way == "c":
            peer = (s, (1 - c) * 2 + d)
            index = (k, fb, 1, fd)
        else:
            peer = (s, c * 2 + 1 - d)
            index = (k, fb, fc, 1)
        number = ((index[0] * 2 + index[1]) * 2 + index[2]) * 2 + index[3]
        source = own(part) if slot == (0, 0, 0, 0) else landing(part, slot)
        copy = pltpu.make_async_remote_copy(
            source,
            landing(part, slot),
            w_send.at[part, number],
            w_recv.at[part, number],
            peer,
            MESH,
        )
        copy.start()
        started.append(copy)

    def arrive(part, slot):
        k, fb, fc, fd = slot
        number = ((k * 2 + fb) * 2 + fc) * 2 + fd
        target = landing(part, slot)
        pltpu.make_async_copy(target, target, w_recv.at[part, number]).wait()

    def onward(part, slot):
        k, fb, fc, fd = slot
        if part == 0:
            if not fb and not fc:
                send(part, slot, "b")
            if not fc:
                send(part, slot, "c")
        else:
            if not fb and not fc:
                send(part, slot, "c")
            if not fb:
                send(part, slot, "b")
        send(part, slot, "d")

    for part in range(2):
        for hop in range(1, deep):
            send(part, (0, 0, 0, 0), "a", hop)
    for part in range(2):
        onward(part, (0, 0, 0, 0))
    local = []
    for part in range(2):
        copy = pltpu.make_async_copy(own(part), landing(part, (0, 0, 0, 0)), own_sem.at[part])
        copy.start()
        local.append(copy)
    share = cond_ref.shape[1] // tp_size
    cond_copies = []
    for j in range(1, tp_size):
        peer = tp_peers[j - 1]
        copy = pltpu.make_async_remote_copy(
            cond_ref.at[:, pl.ds(pl.multiple_of(peer[1] * share, share), share), :],
            cond_out.at[t],
            c_send.at[j],
            c_recv.at[tp_size - j],
            peer,
            MESH,
        )
        copy.start()
        cond_copies.append(copy)
    copy = pltpu.make_async_copy(
        cond_ref.at[:, pl.ds(pl.multiple_of(t * share, share), share), :],
        cond_out.at[t],
        own_sem.at[2],
    )
    copy.start()
    local.append(copy)

    asked[s] = req_ref[s]
    for copy in requests:
        copy.wait()
    places = asked[...].reshape(seq_size * 8, 128)[:, :1]
    stored = tok_ref.shape[0]
    pick = (
        lax.broadcasted_iota(jnp.int32, (seq_size * 8, stored), 1) == places
    ).astype(jnp.float32).astype(jnp.bfloat16)

    def chosen(values):
        return jnp.dot(
            pick,
            values.astype(jnp.float32).astype(jnp.bfloat16),
            preferred_element_type=jnp.float32,
        )

    tokens = tok_ref[...]
    high = tokens >> 7
    found = chosen(high) * 128.0 + chosen(tokens - (high << 7))
    answer[:, :, 0:128] = found.astype(jnp.int32).reshape(seq_size, 8, 128)
    answer[:, :, 128:256] = chosen(dep_ref[...]).astype(jnp.int32).reshape(seq_size, 8, 128)
    answer[:, :, 256:384] = chosen(par_ref[...]).astype(jnp.int32).reshape(seq_size, 8, 128)
    answers = []
    for j in range(1, seq_size):
        peer = seq_peers[j - 1]
        copy = pltpu.make_async_remote_copy(
            answer.at[peer[0]], resp_ref.at[s], r_send.at[j], r_recv.at[seq_size - j], peer, MESH
        )
        copy.start()
        answers.append(copy)
    resp_ref[s] = answer[s]

    for step in range(deep + 2):
        for k, group in (
            (step, ((0, 0),)),
            (step - 1, ((1, 0), (0, 1))),
            (step - 2, ((1, 1),)),
        ):
            if 0 <= k < deep:
                for part in range(2):
                    for fb, fc in group if part == 0 else group[::-1]:
                        slot = (k, fb, fc, 0)
                        if slot != (0, 0, 0, 0):
                            arrive(part, slot)
                            onward(part, slot)
    for k in range(deep):
        for fb in range(2):
            for fc in range(2):
                for part in range(2):
                    arrive(part, (k, fb, fc, 1))
    for copy in answers + cond_copies + local:
        copy.wait()
    for copy in started:
        copy.wait_send()


def swap_kernel(tp_size, emb_ref, out_ref, send_sem, recv_sem, own_sem):
    s, t = lax.axis_index("seq"), lax.axis_index("tp")
    share = emb_ref.shape[0] // tp_size
    peers = [(s, lax.rem(t + j, tp_size)) for j in range(1, tp_size)]
    enter(peers)
    copies = []
    for j in range(1, tp_size):
        peer = peers[j - 1]
        copy = pltpu.make_async_remote_copy(
            emb_ref.at[pl.ds(pl.multiple_of(peer[1] * share, share), share), :],
            out_ref.at[t],
            send_sem.at[j],
            recv_sem.at[tp_size - j],
            peer,
            MESH,
        )
        copy.start()
        copies.append(copy)
    copy = pltpu.make_async_copy(
        emb_ref.at[pl.ds(pl.multiple_of(t * share, share), share), :], out_ref.at[t], own_sem
    )
    copy.start()
    copy.wait()
    for copy in copies:
        copy.wait()


def spread_kernel(seq_size, tp_size, kv_ref, out_ref, send_sem, recv_sem, carry_send, carry_recv, own_sem):
    s, t = lax.axis_index("seq"), lax.axis_index("tp")
    share = kv_ref.shape[1]
    lead = out_ref.shape[0] - share * tp_size
    gives = jnp.logical_and(t == tp_size - 1, s < seq_size - 1)
    takes = s > 0
    peers = [(s, lax.rem(t + j, tp_size)) for j in range(1, tp_size)]
    barrier = pltpu.get_barrier_semaphore()
    for peer in peers:
        pl.semaphore_signal(barrier, inc=1, device_id=peer, device_id_type=MESH)

    @pl.when(takes)
    def _():
        pl.semaphore_signal(
            barrier, inc=1, device_id=(s - 1, jnp.int32(tp_size - 1)), device_id_type=MESH
        )

    @pl.when(gives)
    def _():
        pl.semaphore_wait(barrier, 2 * tp_size - 1)

    @pl.when(jnp.logical_not(gives))
    def _():
        pl.semaphore_wait(barrier, tp_size - 1)

    def mine():
        return out_ref.at[pl.ds(pl.multiple_of(lead + t * share, lead), share), :]

    copies = []
    for j in range(1, tp_size):
        peer = peers[j - 1]
        copy = pltpu.make_async_remote_copy(
            kv_ref.at[peer[1]], mine(), send_sem.at[j], recv_sem.at[tp_size - j], peer, MESH
        )
        copy.start()
        copies.append(copy)

    def carry(p):
        return pltpu.make_async_remote_copy(
            kv_ref.at[p, pl.ds(share - lead, lead), :],
            out_ref.at[pl.ds(0, lead), :],
            carry_send.at[p],
            carry_recv,
            (s + 1, jnp.int32(p)),
            MESH,
        )

    @pl.when(gives)
    def _():
        for p in range(tp_size):
            carry(p).start()

    copy = pltpu.make_async_copy(kv_ref.at[t], mine(), own_sem)
    copy.start()
    copy.wait()
    for copy in copies:
        copy.wait()

    @pl.when(gives)
    def _():
        for p in range(tp_size):
            carry(p).wait_send()

    @pl.when(takes)
    def _():
        target = out_ref.at[pl.ds(0, lead), :]
        pltpu.make_async_copy(target, target, carry_recv).wait()


def encoder_kernel(
    tp_size, length, pairs, bias_ref, emb_ref, gain_ref, w_ref, cca_ref, cond_ref, hit_ref, kv_ref, normed, total, q_s, k_s, v_s, mixed
):
    step = pl.program_id(0)
    rows, width = normed.shape
    part = width // tp_size
    blocks = cond_ref.shape[2]
    cond_len = cond_ref.shape[3]

    @pl.when(step == 0)
    def _():
        square = jnp.zeros((rows, 1), jnp.float32)
        for p in range(tp_size):
            piece = emb_ref[p].astype(jnp.float32)
            square += jnp.sum(piece * piece, axis=-1, keepdims=True)
        factor = lax.rsqrt(square * (1.0 / width) + 1e-05)
        for p in range(tp_size):
            columns = slice(p * part, (p + 1) * part)
            normed[:, columns] = (
                emb_ref[p].astype(jnp.float32) * factor * gain_ref[:, columns]
            ).astype(jnp.bfloat16)
            total[:, columns] = emb_ref[p].astype(jnp.float32)

    hidden = normed[...]
    for m, target in ((0, q_s), (1, k_s), (2, v_s)):
        target[...] = jnp.dot(
            hidden, w_ref[0, m], preferred_element_type=jnp.float32
        ).astype(jnp.bfloat16)
    for h in range(part // HD):
        columns = slice(h * HD, (h + 1) * HD)
        bias = bias_ref[step * (part // HD) + h]
        for c in range(blocks):
            cond_k = cond_ref[0, 0, c, :, columns]
            cond_v = cond_ref[0, 1, c, :, columns]
            for k in range(pairs):
                unit = c * pairs + k
                span = slice(unit * length, (unit + 1) * length)
                query = q_s[span, columns]
                near = lax.dot_general(
                    query, k_s[span, columns], NT, preferred_element_type=jnp.float32
                ) * SCALE + bias * hit_ref[unit]
                far = lax.dot_general(
                    query, cond_k, NT, preferred_element_type=jnp.float32
                ) * SCALE
                top = jnp.maximum(
                    jnp.max(near, axis=-1, keepdims=True), jnp.max(far, axis=-1, keepdims=True)
                )
                near, far = jnp.exp(near - top), jnp.exp(far - top)
                share = 1.0 / (
                    jnp.sum(near, axis=-1, keepdims=True) + jnp.sum(far, axis=-1, keepdims=True)
                )
                result = jnp.dot(
                    (near * share).astype(jnp.bfloat16),
                    v_s[span, columns],
                    preferred_element_type=jnp.float32,
                ) + jnp.dot(
                    (far * share).astype(jnp.bfloat16), cond_v, preferred_element_type=jnp.float32
                )
                mixed[span, columns] = result.astype(jnp.bfloat16)
    total[...] += lax.dot_general(
        mixed[...], w_ref[0, 3], NT, preferred_element_type=jnp.float32
    )

    @pl.when(step == tp_size - 1)
    def _():
        encoded = total[...].astype(jnp.bfloat16)
        for p in range(tp_size):
            kv_ref[p] = jnp.dot(
                encoded, cca_ref[p, 0], preferred_element_type=jnp.float32
            ).astype(jnp.bfloat16)


def softmax_rows(scores):
    scores = jnp.exp(scores - jnp.max(scores, axis=-1, keepdims=True))
    return (scores * (1.0 / jnp.sum(scores, axis=-1, keepdims=True))).astype(jnp.bfloat16)


def attend_kernel(allowed_ref, q_ref, prev_ref, cur_ref, out_ref):
    block = pl.program_id(0)
    tokens = q_ref.shape[0]
    heads = q_ref.shape[1] // HD
    query = q_ref[...]
    stacked = jnp.concatenate([query[:, h * HD : (h + 1) * HD] for h in range(heads)], axis=0)
    ok = allowed_ref[block] > 0

    def mix(rows, kv_ref):
        scores = lax.dot_general(
            rows, kv_ref[:, :HD], NT, preferred_element_type=jnp.float32
        ) * SCALE
        return jnp.dot(
            softmax_rows(scores), kv_ref[:, HD:], preferred_element_type=jnp.float32
        )

    leading = mix(stacked, prev_ref)
    tail = query[tokens - 16 :, :]
    tails = jnp.concatenate([tail[:, h * HD : (h + 1) * HD] for h in range(heads)], axis=0)
    trailing = mix(tails, cur_ref)
    last = lax.broadcasted_iota(jnp.int32, (16, HD), 0) == 15
    for h in range(heads):
        columns = slice(h * HD, (h + 1) * HD)
        value = leading[h * tokens : (h + 1) * tokens]
        value = jnp.where(ok, value, jnp.zeros_like(value))
        out_ref[: tokens - 16, columns] = value[: tokens - 16].astype(jnp.bfloat16)
        out_ref[tokens - 16 :, columns] = jnp.where(
            last, trailing[h * 16 : (h + 1) * 16], value[tokens - 16 :]
        ).astype(jnp.bfloat16)


def shards(
    db_tokens,
    db_parent,
    db_depth,
    nb_rows,
    seq_start,
    table,
    depth_table,
    enc_gain,
    enc_qkv,
    tree_bias,
    enc_wo,
    cond_kv,
    queries,
    cca_kv,
):
    seq_size = lax.axis_size("seq")
    tp_size = lax.axis_size("tp")
    block_count, pair_count = nb_rows.shape
    unit_count = block_count * pair_count
    stored, length = db_tokens.shape
    slot_count = max(1, 2 * unit_count // seq_size)
    part = enc_qkv.shape[2]
    rows = enc_qkv.shape[0]
    width = part * tp_size
    cond_len = cond_kv.shape[0] // block_count
    bf16 = jnp.bfloat16
    anywhere = pl.BlockSpec(memory_space=pl.ANY)
    vmem = pl.BlockSpec(memory_space=pltpu.VMEM)
    dma = pltpu.SemaphoreType.DMA

    flat_rows = nb_rows.reshape(unit_count)
    holder = flat_rows // stored
    local_row = flat_rows % stored
    ordering = jnp.arange(unit_count, dtype=jnp.int32)
    earlier = jnp.sum(
        ((holder[:, None] == holder[None, :]) & (ordering[:, None] > ordering[None, :])).astype(
            jnp.int32
        ),
        axis=1,
    )
    target = holder * 8 + earlier
    places = jnp.arange(seq_size * 8, dtype=jnp.int32)
    request = jnp.sum(
        jnp.where(target[None, :] == places[:, None], local_row[None, :], 0), axis=1
    )
    request = jnp.broadcast_to(request.reshape(seq_size, 8, 1), (seq_size, 8, 128))
    packed = jnp.concatenate(
        [
            enc_qkv.transpose(1, 0, 2),
            enc_wo.T[None],
            cca_kv.reshape(1, rows, part),
        ],
        axis=0,
    )
    cond = cond_kv.transpose(1, 0, 2)
    share = unit_count // tp_size
    block_share = block_count // tp_size
    full, response, own_cond = pl.pallas_call(
        functools.partial(gather_kernel, seq_size, tp_size),
        out_shape=(
            jax.ShapeDtypeStruct((tp_size, 5, width, part), bf16),
            jax.ShapeDtypeStruct((seq_size, 8, 384), jnp.int32),
            jax.ShapeDtypeStruct((tp_size, 2, block_share * cond_len, part), bf16),
        ),
        in_specs=[vmem] * 4 + [anywhere] * 2,
        out_specs=(anywhere, vmem, anywhere),
        scratch_shapes=[
            pltpu.VMEM((seq_size, 8, 128), jnp.int32),
            pltpu.VMEM((seq_size, 8, 384), jnp.int32),
            dma((2, seq_size * tp_size)),
            dma((2, seq_size * tp_size)),
            dma((3,)),
            dma((seq_size,)),
            dma((seq_size,)),
            dma((seq_size,)),
            dma((seq_size,)),
            dma((tp_size,)),
            dma((tp_size,)),
        ],
        compiler_params=pltpu.CompilerParams(
            collective_id=0, has_side_effects=True, vmem_limit_bytes=32 << 20
        ),
        name="gather_weights_and_rows",
    )(request, db_tokens, db_depth, db_parent, packed, cond)

    answer = jnp.take(response.reshape(seq_size * 8, 384), target, axis=0, mode="clip")
    tokens = answer[:, :length].reshape(unit_count * length)
    depths = answer[:, length : 2 * length].reshape(unit_count * length)
    parents = lax.dynamic_slice_in_dim(
        answer[:, 2 * length :], lax.axis_index("tp") * share, share, 0
    )
    hit = (parents[:, :, None] == jnp.arange(length, dtype=jnp.int32)).astype(jnp.float32)
    depth_pick = (
        depths[:, None] == jnp.arange(depth_table.shape[0], dtype=jnp.int32)[None, :]
    ).astype(bf16)
    embedded = (
        jnp.take(table, tokens, axis=0, mode="clip").astype(jnp.float32)
        + jnp.dot(depth_pick, depth_table, preferred_element_type=jnp.float32)
    ).astype(bf16)

    mine = share * length
    own_emb = pl.pallas_call(
        functools.partial(swap_kernel, tp_size),
        out_shape=jax.ShapeDtypeStruct((tp_size, mine, part), bf16),
        in_specs=[anywhere],
        out_specs=anywhere,
        scratch_shapes=[dma((tp_size,)), dma((tp_size,)), dma],
        compiler_params=pltpu.CompilerParams(collective_id=1, has_side_effects=True),
        name="swap_embedded_columns",
    )(embedded)

    cond_blocks = own_cond.reshape(tp_size, 2, block_share, cond_len, part)
    keys_values = pl.pallas_call(
        functools.partial(encoder_kernel, tp_size, length, pair_count),
        grid=(tp_size,),
        out_shape=jax.ShapeDtypeStruct((tp_size, mine, part), bf16),
        in_specs=[
            pl.BlockSpec(memory_space=pltpu.SMEM),
            pl.BlockSpec((tp_size, mine, part), lambda i: (0, 0, 0)),
            pl.BlockSpec((1, width), lambda i: (0, 0)),
            pl.BlockSpec((1, 4, width, part), lambda i: (i, 0, 0, 0)),
            pl.BlockSpec((tp_size, 1, width, part), lambda i: (0, 4, 0, 0)),
            pl.BlockSpec((1, 2, block_share, cond_len, part), lambda i: (i, 0, 0, 0, 0)),
            pl.BlockSpec((share, length, length), lambda i: (0, 0, 0)),
        ],
        out_specs=pl.BlockSpec((tp_size, mine, part), lambda i: (0, 0, 0)),
        scratch_shapes=[
            pltpu.VMEM((mine, width), bf16),
            pltpu.VMEM((mine, width), jnp.float32),
            pltpu.VMEM((mine, part), bf16),
            pltpu.VMEM((mine, part), bf16),
            pltpu.VMEM((mine, part), bf16),
            pltpu.VMEM((mine, part), bf16),
        ],
        compiler_params=pltpu.CompilerParams(vmem_limit_bytes=48 << 20),
        name="encode",
    )(tree_bias, own_emb, enc_gain.reshape(1, width), full, full, cond_blocks, hit)

    key_rows = pair_count * length
    spread = pl.pallas_call(
        functools.partial(spread_kernel, seq_size, tp_size),
        out_shape=jax.ShapeDtypeStruct(((block_count + 1) * key_rows, part), bf16),
        in_specs=[anywhere],
        out_specs=anywhere,
        scratch_shapes=[dma((tp_size,)), dma((tp_size,)), dma((tp_size,)), dma, dma],
        compiler_params=pltpu.CompilerParams(collective_id=2, has_side_effects=True),
        name="spread_keys_values",
    )(keys_values)

    block_index = lax.axis_index("seq") * block_count + jnp.arange(block_count, dtype=jnp.int32)
    allowed = ((block_index > 0) & (seq_start == 0)).astype(jnp.int32)
    columns = queries.shape[1]
    return pl.pallas_call(
        attend_kernel,
        grid=(block_count,),
        out_shape=jax.ShapeDtypeStruct(queries.shape, bf16),
        in_specs=[
            pl.BlockSpec(memory_space=pltpu.SMEM),
            pl.BlockSpec((cond_len, columns), lambda i: (i, 0)),
            pl.BlockSpec((key_rows, part), lambda i: (i, 0)),
            pl.BlockSpec((key_rows, part), lambda i: (i + 1, 0)),
        ],
        out_specs=pl.BlockSpec((cond_len, columns), lambda i: (i, 0)),
        compiler_params=pltpu.CompilerParams(vmem_limit_bytes=32 << 20),
        name="attend",
    )(allowed, queries, spread, spread)


def solution(mesh):
    in_specs = (
        P("seq", None),
        P("seq", None),
        P("seq", None),
        P("seq", None),
        P("seq"),
        P(None, "tp"),
        P(None, "tp"),
        P(),
        P("seq", None, "tp"),
        P(),
        P("tp", "seq"),
        P("seq", None, "tp"),
        P("seq", "tp"),
        P("seq", None, "tp"),
    )
    out_specs = P("seq", "tp")
    return jax.shard_map(shards, mesh=mesh, in_specs=in_specs, out_specs=out_specs, check_vma=False)
```

```python
import functools
import math

import jax
import jax.numpy as jnp
from jax import lax
from jax.experimental import pallas as pl
from jax.experimental.pallas import tpu as pltpu
from jax.sharding import PartitionSpec as P

HD = 128
SCALE = 1.0 / math.sqrt(HD)
MESH = pl.DeviceIdType.MESH
PARTS = ((0, 2), (2, 3))
NT = (((1,), (1,)), ((), ()))


def enter(peers):
    barrier = pltpu.get_barrier_semaphore()
    for peer in peers:
        pl.semaphore_signal(barrier, inc=1, device_id=peer, device_id_type=MESH)
    pl.semaphore_wait(barrier, len(peers))


def fetch_kernel(
    seq_size, tp_size, req_ref, tok_ref, dep_ref, par_ref, cond_ref, resp_ref, cond_out, asked, answer, own_sem, q_send, q_recv, r_send, r_recv, c_send, c_recv
):
    s, t = lax.axis_index("seq"), lax.axis_index("tp")
    seq_peers = [(lax.rem(s + j, seq_size), t) for j in range(1, seq_size)]
    tp_peers = [(s, lax.rem(t + j, tp_size)) for j in range(1, tp_size)]
    enter(seq_peers + tp_peers)
    requests = []
    for j in range(1, seq_size):
        peer = seq_peers[j - 1]
        copy = pltpu.make_async_remote_copy(
            req_ref.at[peer[0]], asked.at[s], q_send.at[j], q_recv.at[seq_size - j], peer, MESH
        )
        copy.start()
        requests.append(copy)

    share = cond_ref.shape[1] // tp_size
    cond_copies = []
    for j in range(1, tp_size):
        peer = tp_peers[j - 1]
        copy = pltpu.make_async_remote_copy(
            cond_ref.at[:, pl.ds(pl.multiple_of(peer[1] * share, share), share), :],
            cond_out.at[t],
            c_send.at[j],
            c_recv.at[tp_size - j],
            peer,
            MESH,
        )
        copy.start()
        cond_copies.append(copy)
    copy = pltpu.make_async_copy(
        cond_ref.at[:, pl.ds(pl.multiple_of(t * share, share), share), :],
        cond_out.at[t],
        own_sem,
    )
    copy.start()
    kept = copy

    asked[s] = req_ref[s]
    for copy in requests:
        copy.wait()
    places = asked[...].reshape(seq_size * 8, 128)[:, :1]
    stored = tok_ref.shape[0]
    pick = (
        lax.broadcasted_iota(jnp.int32, (seq_size * 8, stored), 1) == places
    ).astype(jnp.float32).astype(jnp.bfloat16)

    def chosen(values):
        return jnp.dot(
            pick,
            values.astype(jnp.float32).astype(jnp.bfloat16),
            preferred_element_type=jnp.float32,
        )

    tokens = tok_ref[...]
    high = tokens >> 7
    found = chosen(high) * 128.0 + chosen(tokens - (high << 7))
    answer[:, :, 0:128] = found.astype(jnp.int32).reshape(seq_size, 8, 128)
    answer[:, :, 128:256] = chosen(dep_ref[...]).astype(jnp.int32).reshape(seq_size, 8, 128)
    answer[:, :, 256:384] = chosen(par_ref[...]).astype(jnp.int32).reshape(seq_size, 8, 128)
    answers = []
    for j in range(1, seq_size):
        peer = seq_peers[j - 1]
        copy = pltpu.make_async_remote_copy(
            answer.at[peer[0]], resp_ref.at[s], r_send.at[j], r_recv.at[seq_size - j], peer, MESH
        )
        copy.start()
        answers.append(copy)
    resp_ref[s] = answer[s]

    for copy in answers + cond_copies + [kept]:
        copy.wait()


def gather_kernel(
    seq_size,
    tp_size,
    w_ref,
    emb_ref,
    full_ref,
    emb_out,
    w_send,
    w_recv,
    own_sem,
    e_send,
    e_recv,
):
    s, t = lax.axis_index("seq"), lax.axis_index("tp")
    deep = seq_size // 2
    rows = w_ref.shape[1]
    seq_peers = [(lax.rem(s + j, seq_size), t) for j in range(1, seq_size)]
    tp_peers = [(s, lax.rem(t + j, tp_size)) for j in range(1, tp_size)]
    enter(seq_peers + tp_peers)

    started = []
    a, b = s // 2, s % 2
    c, d = t // 2, t % 2

    def place(slot):
        k, fb, fc, fd = slot
        sa = lax.rem(a + k, deep)
        sb = 1 - b if fb else b
        sc = 1 - c if fc else c
        sd = 1 - d if fd else d
        return sa * 2 + sb, sc * 2 + sd

    def landing(part, slot):
        ps, pt = place(slot)
        first, count = PARTS[part]
        return full_ref.at[
            pt, pl.ds(first, count), pl.ds(pl.multiple_of(ps * rows, rows), rows), :
        ]

    def own(part):
        first, count = PARTS[part]
        return w_ref.at[pl.ds(first, count)]

    def send(part, slot, way, hop=0):
        k, fb, fc, fd = slot
        if way == "a":
            peer = (lax.rem(a + hop, deep) * 2 + b, t)
            index = ((deep - hop) % deep, fb, fc, fd)
        elif way == "b":
            peer = (a * 2 + 1 - b, t)
            index = (k, 1, fc, fd)
        elif way == "c":
            peer = (s, (1 - c) * 2 + d)
            index = (k, fb, 1, fd)
        else:
            peer = (s, c * 2 + 1 - d)
            index = (k, fb, fc, 1)
        number = ((index[0] * 2 + index[1]) * 2 + index[2]) * 2 + index[3]
        source = own(part) if slot == (0, 0, 0, 0) else landing(part, slot)
        copy = pltpu.make_async_remote_copy(
            source,
            landing(part, slot),
            w_send.at[part, number],
            w_recv.at[part, number],
            peer,
            MESH,
        )
        copy.start()
        started.append(copy)

    def arrive(part, slot):
        k, fb, fc, fd = slot
        number = ((k * 2 + fb) * 2 + fc) * 2 + fd
        target = landing(part, slot)
        pltpu.make_async_copy(target, target, w_recv.at[part, number]).wait()

    def onward(part, slot):
        k, fb, fc, fd = slot
        if part == 0:
            if not fb and not fc:
                send(part, slot, "b")
            if not fc:
                send(part, slot, "c")
        else:
            if not fb and not fc:
                send(part, slot, "c")
            if not fb:
                send(part, slot, "b")
        send(part, slot, "d")

    for part in range(2):
        for hop in range(1, deep):
            send(part, (0, 0, 0, 0), "a", hop)
    for part in range(2):
        onward(part, (0, 0, 0, 0))
    local = []
    for part in range(2):
        copy = pltpu.make_async_copy(own(part), landing(part, (0, 0, 0, 0)), own_sem.at[part])
        copy.start()
        local.append(copy)
    share = emb_ref.shape[0] // tp_size
    emb_copies = []
    for j in range(1, tp_size):
        peer = tp_peers[j - 1]
        copy = pltpu.make_async_remote_copy(
            emb_ref.at[pl.ds(pl.multiple_of(peer[1] * share, share), share), :],
            emb_out.at[t],
            e_send.at[j],
            e_recv.at[tp_size - j],
            peer,
            MESH,
        )
        copy.start()
        emb_copies.append(copy)
    copy = pltpu.make_async_copy(
        emb_ref.at[pl.ds(pl.multiple_of(t * share, share), share), :],
        emb_out.at[t],
        own_sem.at[2],
    )
    copy.start()
    local.append(copy)

    for step in range(deep + 2):
        for k, group in (
            (step, ((0, 0),)),
            (step - 1, ((1, 0), (0, 1))),
            (step - 2, ((1, 1),)),
        ):
            if 0 <= k < deep:
                for part in range(2):
                    for fb, fc in group if part == 0 else group[::-1]:
                        slot = (k, fb, fc, 0)
                        if slot != (0, 0, 0, 0):
                            arrive(part, slot)
                            onward(part, slot)
    for k in range(deep):
        for fb in range(2):
            for fc in range(2):
                for part in range(2):
                    arrive(part, (k, fb, fc, 1))
    for copy in emb_copies + local:
        copy.wait()
    for copy in started:
        copy.wait_send()


def spread_kernel(seq_size, tp_size, kv_ref, out_ref, send_sem, recv_sem, carry_send, carry_recv, own_sem):
    s, t = lax.axis_index("seq"), lax.axis_index("tp")
    share = kv_ref.shape[1]
    lead = out_ref.shape[0] - share * tp_size
    gives = jnp.logical_and(t == tp_size - 1, s < seq_size - 1)
    takes = s > 0
    peers = [(s, lax.rem(t + j, tp_size)) for j in range(1, tp_size)]
    barrier = pltpu.get_barrier_semaphore()
    for peer in peers:
        pl.semaphore_signal(barrier, inc=1, device_id=peer, device_id_type=MESH)

    @pl.when(takes)
    def _():
        pl.semaphore_signal(
            barrier, inc=1, device_id=(s - 1, jnp.int32(tp_size - 1)), device_id_type=MESH
        )

    @pl.when(gives)
    def _():
        pl.semaphore_wait(barrier, 2 * tp_size - 1)

    @pl.when(jnp.logical_not(gives))
    def _():
        pl.semaphore_wait(barrier, tp_size - 1)

    def mine():
        return out_ref.at[pl.ds(pl.multiple_of(lead + t * share, lead), share), :]

    copies = []
    for j in range(1, tp_size):
        peer = peers[j - 1]
        copy = pltpu.make_async_remote_copy(
            kv_ref.at[peer[1]], mine(), send_sem.at[j], recv_sem.at[tp_size - j], peer, MESH
        )
        copy.start()
        copies.append(copy)

    def carry(p):
        return pltpu.make_async_remote_copy(
            kv_ref.at[p, pl.ds(share - lead, lead), :],
            out_ref.at[pl.ds(0, lead), :],
            carry_send.at[p],
            carry_recv,
            (s + 1, jnp.int32(p)),
            MESH,
        )

    @pl.when(gives)
    def _():
        for p in range(tp_size):
            carry(p).start()

    copy = pltpu.make_async_copy(kv_ref.at[t], mine(), own_sem)
    copy.start()
    copy.wait()
    for copy in copies:
        copy.wait()

    @pl.when(gives)
    def _():
        for p in range(tp_size):
            carry(p).wait_send()

    @pl.when(takes)
    def _():
        target = out_ref.at[pl.ds(0, lead), :]
        pltpu.make_async_copy(target, target, carry_recv).wait()


def encoder_kernel(
    tp_size, length, pairs, bias_ref, emb_ref, gain_ref, w_ref, cca_ref, cond_ref, hit_ref, kv_ref, normed, total, q_s, k_s, v_s, mixed
):
    step = pl.program_id(0)
    rows, width = normed.shape
    part = width // tp_size
    blocks = cond_ref.shape[2]
    cond_len = cond_ref.shape[3]

    @pl.when(step == 0)
    def _():
        square = jnp.zeros((rows, 1), jnp.float32)
        for p in range(tp_size):
            piece = emb_ref[p].astype(jnp.float32)
            square += jnp.sum(piece * piece, axis=-1, keepdims=True)
        factor = lax.rsqrt(square * (1.0 / width) + 1e-05)
        for p in range(tp_size):
            columns = slice(p * part, (p + 1) * part)
            normed[:, columns] = (
                emb_ref[p].astype(jnp.float32) * factor * gain_ref[:, columns]
            ).astype(jnp.bfloat16)
            total[:, columns] = emb_ref[p].astype(jnp.float32)

    hidden = normed[...]
    for m, target in ((0, q_s), (1, k_s), (2, v_s)):
        target[...] = jnp.dot(
            hidden, w_ref[0, m], preferred_element_type=jnp.float32
        ).astype(jnp.bfloat16)
    jobs = [
        (h, c, c * pairs + k)
        for h in range(part // HD)
        for c in range(blocks)
        for k in range(pairs)
    ]

    def span_of(h, unit):
        return slice(unit * length, (unit + 1) * length), slice(h * HD, (h + 1) * HD)

    scores = []
    for h, c, unit in jobs:
        span, columns = span_of(h, unit)
        query = q_s[span, columns]
        near = lax.dot_general(query, k_s[span, columns], NT, preferred_element_type=jnp.float32)
        far = lax.dot_general(
            query, cond_ref[0, 0, c, :, columns], NT, preferred_element_type=jnp.float32
        )
        bias = bias_ref[step * (part // HD) + h]
        scores.append((near * SCALE + bias * hit_ref[unit], far * SCALE))
    tops = [
        jnp.maximum(
            jnp.max(near, axis=-1, keepdims=True), jnp.max(far, axis=-1, keepdims=True)
        )
        for near, far in scores
    ]
    scores = [(jnp.exp(near - top), jnp.exp(far - top)) for (near, far), top in zip(scores, tops)]
    shares = [
        1.0 / (jnp.sum(near, axis=-1, keepdims=True) + jnp.sum(far, axis=-1, keepdims=True))
        for near, far in scores
    ]
    results = []
    for (h, c, unit), (near, far), share in zip(jobs, scores, shares):
        span, columns = span_of(h, unit)
        results.append(
            jnp.dot(
                (near * share).astype(jnp.bfloat16),
                v_s[span, columns],
                preferred_element_type=jnp.float32,
            )
            + jnp.dot(
                (far * share).astype(jnp.bfloat16),
                cond_ref[0, 1, c, :, columns],
                preferred_element_type=jnp.float32,
            )
        )
    for (h, c, unit), result in zip(jobs, results):
        span, columns = span_of(h, unit)
        mixed[span, columns] = result.astype(jnp.bfloat16)
    total[...] += lax.dot_general(
        mixed[...], w_ref[0, 3], NT, preferred_element_type=jnp.float32
    )

    @pl.when(step == tp_size - 1)
    def _():
        encoded = total[...].astype(jnp.bfloat16)
        for p in range(tp_size):
            kv_ref[p] = jnp.dot(
                encoded, cca_ref[p, 0], preferred_element_type=jnp.float32
            ).astype(jnp.bfloat16)


def softmax_rows(scores):
    scores = jnp.exp(scores - jnp.max(scores, axis=-1, keepdims=True))
    return (scores * (1.0 / jnp.sum(scores, axis=-1, keepdims=True))).astype(jnp.bfloat16)


def attend_kernel(allowed_ref, q_ref, prev_ref, cur_ref, out_ref):
    block = pl.program_id(0)
    tokens = q_ref.shape[0]
    heads = q_ref.shape[1] // HD
    query = q_ref[...]
    stacked = jnp.concatenate([query[:, h * HD : (h + 1) * HD] for h in range(heads)], axis=0)
    ok = allowed_ref[block] > 0

    def mix(rows, kv_ref):
        scores = lax.dot_general(
            rows, kv_ref[:, :HD], NT, preferred_element_type=jnp.float32
        ) * SCALE
        return jnp.dot(
            softmax_rows(scores), kv_ref[:, HD:], preferred_element_type=jnp.float32
        )

    leading = mix(stacked, prev_ref)
    tail = query[tokens - 16 :, :]
    tails = jnp.concatenate([tail[:, h * HD : (h + 1) * HD] for h in range(heads)], axis=0)
    trailing = mix(tails, cur_ref)
    last = lax.broadcasted_iota(jnp.int32, (16, HD), 0) == 15
    for h in range(heads):
        columns = slice(h * HD, (h + 1) * HD)
        value = leading[h * tokens : (h + 1) * tokens]
        value = jnp.where(ok, value, jnp.zeros_like(value))
        out_ref[: tokens - 16, columns] = value[: tokens - 16].astype(jnp.bfloat16)
        out_ref[tokens - 16 :, columns] = jnp.where(
            last, trailing[h * 16 : (h + 1) * 16], value[tokens - 16 :]
        ).astype(jnp.bfloat16)


def shards(
    db_tokens,
    db_parent,
    db_depth,
    nb_rows,
    seq_start,
    table,
    depth_table,
    enc_gain,
    enc_qkv,
    tree_bias,
    enc_wo,
    cond_kv,
    queries,
    cca_kv,
):
    seq_size = lax.axis_size("seq")
    tp_size = lax.axis_size("tp")
    block_count, pair_count = nb_rows.shape
    unit_count = block_count * pair_count
    stored, length = db_tokens.shape
    slot_count = max(1, 2 * unit_count // seq_size)
    part = enc_qkv.shape[2]
    rows = enc_qkv.shape[0]
    width = part * tp_size
    cond_len = cond_kv.shape[0] // block_count
    bf16 = jnp.bfloat16
    anywhere = pl.BlockSpec(memory_space=pl.ANY)
    vmem = pl.BlockSpec(memory_space=pltpu.VMEM)
    dma = pltpu.SemaphoreType.DMA

    flat_rows = nb_rows.reshape(unit_count)
    holder = flat_rows // stored
    local_row = flat_rows % stored
    ordering = jnp.arange(unit_count, dtype=jnp.int32)
    earlier = jnp.sum(
        ((holder[:, None] == holder[None, :]) & (ordering[:, None] > ordering[None, :])).astype(
            jnp.int32
        ),
        axis=1,
    )
    target = holder * 8 + earlier
    places = jnp.arange(seq_size * 8, dtype=jnp.int32)
    request = jnp.sum(
        jnp.where(target[None, :] == places[:, None], local_row[None, :], 0), axis=1
    )
    request = jnp.broadcast_to(request.reshape(seq_size, 8, 1), (seq_size, 8, 128))
    packed = jnp.concatenate(
        [
            enc_qkv.transpose(1, 0, 2),
            enc_wo.T[None],
            cca_kv.reshape(1, rows, part),
        ],
        axis=0,
    )
    cond = cond_kv.transpose(1, 0, 2)
    share = unit_count // tp_size
    block_share = block_count // tp_size
    response, own_cond = pl.pallas_call(
        functools.partial(fetch_kernel, seq_size, tp_size),
        out_shape=(
            jax.ShapeDtypeStruct((seq_size, 8, 384), jnp.int32),
            jax.ShapeDtypeStruct((tp_size, 2, block_share * cond_len, part), bf16),
        ),
        in_specs=[vmem] * 4 + [anywhere],
        out_specs=(vmem, anywhere),
        scratch_shapes=[
            pltpu.VMEM((seq_size, 8, 128), jnp.int32),
            pltpu.VMEM((seq_size, 8, 384), jnp.int32),
            dma,
            dma((seq_size,)),
            dma((seq_size,)),
            dma((seq_size,)),
            dma((seq_size,)),
            dma((tp_size,)),
            dma((tp_size,)),
        ],
        compiler_params=pltpu.CompilerParams(
            collective_id=0, has_side_effects=True, vmem_limit_bytes=12 << 20
        ),
        name="fetch_rows",
    )(request, db_tokens, db_depth, db_parent, cond)

    answer = jnp.take(response.reshape(seq_size * 8, 384), target, axis=0, mode="clip")
    tokens = answer[:, :length].reshape(unit_count * length)
    depths = answer[:, length : 2 * length].reshape(unit_count * length)
    parents = lax.dynamic_slice_in_dim(
        answer[:, 2 * length :], lax.axis_index("tp") * share, share, 0
    )
    hit = (parents[:, :, None] == jnp.arange(length, dtype=jnp.int32)).astype(jnp.float32)
    depth_pick = (
        depths[:, None] == jnp.arange(depth_table.shape[0], dtype=jnp.int32)[None, :]
    ).astype(bf16)
    embedded = (
        jnp.take(table, tokens, axis=0, mode="clip").astype(jnp.float32)
        + jnp.dot(depth_pick, depth_table, preferred_element_type=jnp.float32)
    ).astype(bf16)

    mine = share * length
    full, own_emb = pl.pallas_call(
        functools.partial(gather_kernel, seq_size, tp_size),
        out_shape=(
            jax.ShapeDtypeStruct((tp_size, 5, width, part), bf16),
            jax.ShapeDtypeStruct((tp_size, mine, part), bf16),
        ),
        in_specs=[anywhere] * 2,
        out_specs=(anywhere, anywhere),
        scratch_shapes=[
            dma((2, seq_size * tp_size)),
            dma((2, seq_size * tp_size)),
            dma((3,)),
            dma((tp_size,)),
            dma((tp_size,)),
        ],
        compiler_params=pltpu.CompilerParams(collective_id=1, has_side_effects=True),
        name="gather_weights_and_embedded",
    )(packed, embedded)

    cond_blocks = own_cond.reshape(tp_size, 2, block_share, cond_len, part)
    keys_values = pl.pallas_call(
        functools.partial(encoder_kernel, tp_size, length, pair_count),
        grid=(tp_size,),
        out_shape=jax.ShapeDtypeStruct((tp_size, mine, part), bf16),
        in_specs=[
            pl.BlockSpec(memory_space=pltpu.SMEM),
            pl.BlockSpec((tp_size, mine, part), lambda i: (0, 0, 0)),
            pl.BlockSpec((1, width), lambda i: (0, 0)),
            pl.BlockSpec((1, 4, width, part), lambda i: (i, 0, 0, 0)),
            pl.BlockSpec((tp_size, 1, width, part), lambda i: (0, 4, 0, 0)),
            pl.BlockSpec((1, 2, block_share, cond_len, part), lambda i: (i, 0, 0, 0, 0)),
            pl.BlockSpec((share, length, length), lambda i: (0, 0, 0)),
        ],
        out_specs=pl.BlockSpec((tp_size, mine, part), lambda i: (0, 0, 0)),
        scratch_shapes=[
            pltpu.VMEM((mine, width), bf16),
            pltpu.VMEM((mine, width), jnp.float32),
            pltpu.VMEM((mine, part), bf16),
            pltpu.VMEM((mine, part), bf16),
            pltpu.VMEM((mine, part), bf16),
            pltpu.VMEM((mine, part), bf16),
        ],
        compiler_params=pltpu.CompilerParams(vmem_limit_bytes=48 << 20),
        name="encode",
    )(tree_bias, own_emb, enc_gain.reshape(1, width), full, full, cond_blocks, hit)

    key_rows = pair_count * length
    spread = pl.pallas_call(
        functools.partial(spread_kernel, seq_size, tp_size),
        out_shape=jax.ShapeDtypeStruct(((block_count + 1) * key_rows, part), bf16),
        in_specs=[anywhere],
        out_specs=anywhere,
        scratch_shapes=[dma((tp_size,)), dma((tp_size,)), dma((tp_size,)), dma, dma],
        compiler_params=pltpu.CompilerParams(collective_id=2, has_side_effects=True),
        name="spread_keys_values",
    )(keys_values)

    block_index = lax.axis_index("seq") * block_count + jnp.arange(block_count, dtype=jnp.int32)
    allowed = ((block_index > 0) & (seq_start == 0)).astype(jnp.int32)
    columns = queries.shape[1]
    return pl.pallas_call(
        attend_kernel,
        grid=(block_count,),
        out_shape=jax.ShapeDtypeStruct(queries.shape, bf16),
        in_specs=[
            pl.BlockSpec(memory_space=pltpu.SMEM),
            pl.BlockSpec((cond_len, columns), lambda i: (i, 0)),
            pl.BlockSpec((key_rows, part), lambda i: (i, 0)),
            pl.BlockSpec((key_rows, part), lambda i: (i + 1, 0)),
        ],
        out_specs=pl.BlockSpec((cond_len, columns), lambda i: (i, 0)),
        compiler_params=pltpu.CompilerParams(vmem_limit_bytes=32 << 20),
        name="attend",
    )(allowed, queries, spread, spread)


def solution(mesh):
    in_specs = (
        P("seq", None),
        P("seq", None),
        P("seq", None),
        P("seq", None),
        P("seq"),
        P(None, "tp"),
        P(None, "tp"),
        P(),
        P("seq", None, "tp"),
        P(),
        P("tp", "seq"),
        P("seq", None, "tp"),
        P("seq", "tp"),
        P("seq", None, "tp"),
    )
    out_specs = P("seq", "tp")
    return jax.shard_map(shards, mesh=mesh, in_specs=in_specs, out_specs=out_specs, check_vma=False)
```

```python
import functools
import math

import jax
import jax.numpy as jnp
from jax import lax
from jax.experimental import pallas as pl
from jax.experimental.pallas import tpu as pltpu
from jax.sharding import PartitionSpec as P

HD = 128
SCALE = 1.0 / math.sqrt(HD)
MESH = pl.DeviceIdType.MESH
PARTS = ((0, 2), (2, 3))
NT = (((1,), (1,)), ((), ()))


def enter(peers):
    barrier = pltpu.get_barrier_semaphore()
    for peer in peers:
        pl.semaphore_signal(barrier, inc=1, device_id=peer, device_id_type=MESH)
    pl.semaphore_wait(barrier, len(peers))


def fetch_kernel(
    seq_size, tp_size, req_ref, tok_hbm, dep_hbm, par_hbm, cond_ref, resp_ref, cond_out, asked, answer, tok_ref, dep_ref, par_ref, load_sem, own_sem, q_send, q_recv, r_send, r_recv, c_send, c_recv
):
    s, t = lax.axis_index("seq"), lax.axis_index("tp")
    loads = []
    for index, (source, held) in enumerate(
        ((tok_hbm, tok_ref), (dep_hbm, dep_ref), (par_hbm, par_ref))
    ):
        copy = pltpu.make_async_copy(source, held, load_sem.at[index])
        copy.start()
        loads.append(copy)
    seq_peers = [(lax.rem(s + j, seq_size), t) for j in range(1, seq_size)]
    tp_peers = [(s, lax.rem(t + j, tp_size)) for j in range(1, tp_size)]
    enter(seq_peers + tp_peers)
    requests = []
    for j in range(1, seq_size):
        peer = seq_peers[j - 1]
        copy = pltpu.make_async_remote_copy(
            req_ref.at[peer[0]], asked.at[s], q_send.at[j], q_recv.at[seq_size - j], peer, MESH
        )
        copy.start()
        requests.append(copy)

    share = cond_ref.shape[1] // tp_size
    cond_copies = []
    for j in range(1, tp_size):
        peer = tp_peers[j - 1]
        copy = pltpu.make_async_remote_copy(
            cond_ref.at[:, pl.ds(pl.multiple_of(peer[1] * share, share), share), :],
            cond_out.at[t],
            c_send.at[j],
            c_recv.at[tp_size - j],
            peer,
            MESH,
        )
        copy.start()
        cond_copies.append(copy)
    copy = pltpu.make_async_copy(
        cond_ref.at[:, pl.ds(pl.multiple_of(t * share, share), share), :],
        cond_out.at[t],
        own_sem,
    )
    copy.start()
    kept = copy

    asked[s] = req_ref[s]
    for copy in requests + loads:
        copy.wait()
    places = asked[...].reshape(seq_size * 8, 128)[:, :1]
    stored = tok_ref.shape[0]
    pick = (
        lax.broadcasted_iota(jnp.int32, (seq_size * 8, stored), 1) == places
    ).astype(jnp.float32).astype(jnp.bfloat16)

    def chosen(values):
        return jnp.dot(
            pick,
            values.astype(jnp.float32).astype(jnp.bfloat16),
            preferred_element_type=jnp.float32,
        )

    tokens = tok_ref[...]
    high = tokens >> 7
    found = chosen(high) * 128.0 + chosen(tokens - (high << 7))
    answer[:, :, 0:128] = found.astype(jnp.int32).reshape(seq_size, 8, 128)
    answer[:, :, 128:256] = chosen(dep_ref[...]).astype(jnp.int32).reshape(seq_size, 8, 128)
    answer[:, :, 256:384] = chosen(par_ref[...]).astype(jnp.int32).reshape(seq_size, 8, 128)
    answers = []
    for j in range(1, seq_size):
        peer = seq_peers[j - 1]
        copy = pltpu.make_async_remote_copy(
            answer.at[peer[0]], resp_ref.at[s], r_send.at[j], r_recv.at[seq_size - j], peer, MESH
        )
        copy.start()
        answers.append(copy)
    resp_ref[s] = answer[s]

    for copy in answers + cond_copies + [kept]:
        copy.wait()


def gather_kernel(
    seq_size,
    tp_size,
    w_ref,
    emb_ref,
    full_ref,
    emb_out,
    w_send,
    w_recv,
    own_sem,
    e_send,
    e_recv,
):
    s, t = lax.axis_index("seq"), lax.axis_index("tp")
    deep = seq_size // 2
    rows = w_ref.shape[1]
    seq_peers = [(lax.rem(s + j, seq_size), t) for j in range(1, seq_size)]
    tp_peers = [(s, lax.rem(t + j, tp_size)) for j in range(1, tp_size)]
    enter(seq_peers + tp_peers)

    started = []
    a, b = s // 2, s % 2
    c, d = t // 2, t % 2

    def place(slot):
        k, fb, fc, fd = slot
        sa = lax.rem(a + k, deep)
        sb = 1 - b if fb else b
        sc = 1 - c if fc else c
        sd = 1 - d if fd else d
        return sa * 2 + sb, sc * 2 + sd

    def landing(part, slot):
        ps, pt = place(slot)
        first, count = PARTS[part]
        return full_ref.at[
            pt, pl.ds(first, count), pl.ds(pl.multiple_of(ps * rows, rows), rows), :
        ]

    def own(part):
        first, count = PARTS[part]
        return w_ref.at[pl.ds(first, count)]

    def send(part, slot, way, hop=0):
        k, fb, fc, fd = slot
        if way == "a":
            peer = (lax.rem(a + hop, deep) * 2 + b, t)
            index = ((deep - hop) % deep, fb, fc, fd)
        elif way == "b":
            peer = (a * 2 + 1 - b, t)
            index = (k, 1, fc, fd)
        elif way == "c":
            peer = (s, (1 - c) * 2 + d)
            index = (k, fb, 1, fd)
        else:
            peer = (s, c * 2 + 1 - d)
            index = (k, fb, fc, 1)
        number = ((index[0] * 2 + index[1]) * 2 + index[2]) * 2 + index[3]
        source = own(part) if slot == (0, 0, 0, 0) else landing(part, slot)
        copy = pltpu.make_async_remote_copy(
            source,
            landing(part, slot),
            w_send.at[part, number],
            w_recv.at[part, number],
            peer,
            MESH,
        )
        copy.start()
        started.append(copy)

    def arrive(part, slot):
        k, fb, fc, fd = slot
        number = ((k * 2 + fb) * 2 + fc) * 2 + fd
        target = landing(part, slot)
        pltpu.make_async_copy(target, target, w_recv.at[part, number]).wait()

    def onward(part, slot):
        k, fb, fc, fd = slot
        if part == 0:
            if not fb and not fc:
                send(part, slot, "b")
            if not fc:
                send(part, slot, "c")
        else:
            if not fb and not fc:
                send(part, slot, "c")
            if not fb:
                send(part, slot, "b")
        send(part, slot, "d")

    for part in range(2):
        for hop in range(1, deep):
            send(part, (0, 0, 0, 0), "a", hop)
    for part in range(2):
        onward(part, (0, 0, 0, 0))
    local = []
    for part in range(2):
        copy = pltpu.make_async_copy(own(part), landing(part, (0, 0, 0, 0)), own_sem.at[part])
        copy.start()
        local.append(copy)
    share = emb_ref.shape[0] // tp_size
    emb_copies = []
    for j in range(1, tp_size):
        peer = tp_peers[j - 1]
        copy = pltpu.make_async_remote_copy(
            emb_ref.at[pl.ds(pl.multiple_of(peer[1] * share, share), share), :],
            emb_out.at[t],
            e_send.at[j],
            e_recv.at[tp_size - j],
            peer,
            MESH,
        )
        copy.start()
        emb_copies.append(copy)
    copy = pltpu.make_async_copy(
        emb_ref.at[pl.ds(pl.multiple_of(t * share, share), share), :],
        emb_out.at[t],
        own_sem.at[2],
    )
    copy.start()
    local.append(copy)

    for step in range(deep + 2):
        for k, group in (
            (step, ((0, 0),)),
            (step - 1, ((1, 0), (0, 1))),
            (step - 2, ((1, 1),)),
        ):
            if 0 <= k < deep:
                for part in range(2):
                    for fb, fc in group if part == 0 else group[::-1]:
                        slot = (k, fb, fc, 0)
                        if slot != (0, 0, 0, 0):
                            arrive(part, slot)
                            onward(part, slot)
    for k in range(deep):
        for fb in range(2):
            for fc in range(2):
                for part in range(2):
                    arrive(part, (k, fb, fc, 1))
    for copy in emb_copies + local:
        copy.wait()
    for copy in started:
        copy.wait_send()


def spread_kernel(seq_size, tp_size, kv_ref, out_ref, send_sem, recv_sem, carry_send, carry_recv, own_sem):
    s, t = lax.axis_index("seq"), lax.axis_index("tp")
    share = kv_ref.shape[1]
    lead = out_ref.shape[0] - share * tp_size
    gives = jnp.logical_and(t == tp_size - 1, s < seq_size - 1)
    takes = s > 0
    peers = [(s, lax.rem(t + j, tp_size)) for j in range(1, tp_size)]
    barrier = pltpu.get_barrier_semaphore()
    for peer in peers:
        pl.semaphore_signal(barrier, inc=1, device_id=peer, device_id_type=MESH)

    @pl.when(takes)
    def _():
        pl.semaphore_signal(
            barrier, inc=1, device_id=(s - 1, jnp.int32(tp_size - 1)), device_id_type=MESH
        )

    @pl.when(gives)
    def _():
        pl.semaphore_wait(barrier, 2 * tp_size - 1)

    @pl.when(jnp.logical_not(gives))
    def _():
        pl.semaphore_wait(barrier, tp_size - 1)

    def mine():
        return out_ref.at[pl.ds(pl.multiple_of(lead + t * share, lead), share), :]

    copies = []
    for j in range(1, tp_size):
        peer = peers[j - 1]
        copy = pltpu.make_async_remote_copy(
            kv_ref.at[peer[1]], mine(), send_sem.at[j], recv_sem.at[tp_size - j], peer, MESH
        )
        copy.start()
        copies.append(copy)

    def carry(p):
        return pltpu.make_async_remote_copy(
            kv_ref.at[p, pl.ds(share - lead, lead), :],
            out_ref.at[pl.ds(0, lead), :],
            carry_send.at[p],
            carry_recv,
            (s + 1, jnp.int32(p)),
            MESH,
        )

    @pl.when(gives)
    def _():
        for p in range(tp_size):
            carry(p).start()

    copy = pltpu.make_async_copy(kv_ref.at[t], mine(), own_sem)
    copy.start()
    copy.wait()
    for copy in copies:
        copy.wait()

    @pl.when(gives)
    def _():
        for p in range(tp_size):
            carry(p).wait_send()

    @pl.when(takes)
    def _():
        target = out_ref.at[pl.ds(0, lead), :]
        pltpu.make_async_copy(target, target, carry_recv).wait()


def encoder_kernel(
    tp_size, length, pairs, bias_ref, emb_ref, gain_ref, w_ref, cca_ref, cond_ref, hit_ref, kv_ref, normed, total, q_s, k_s, v_s, mixed
):
    step = pl.program_id(0)
    rows, width = normed.shape
    part = width // tp_size
    blocks = cond_ref.shape[2]
    cond_len = cond_ref.shape[3]

    @pl.when(step == 0)
    def _():
        square = jnp.zeros((rows, 1), jnp.float32)
        for p in range(tp_size):
            piece = emb_ref[p].astype(jnp.float32)
            square += jnp.sum(piece * piece, axis=-1, keepdims=True)
        factor = lax.rsqrt(square * (1.0 / width) + 1e-05)
        for p in range(tp_size):
            columns = slice(p * part, (p + 1) * part)
            normed[:, columns] = (
                emb_ref[p].astype(jnp.float32) * factor * gain_ref[:, columns]
            ).astype(jnp.bfloat16)
            total[:, columns] = emb_ref[p].astype(jnp.float32)

    hidden = normed[...]
    for m, target in ((0, q_s), (1, k_s), (2, v_s)):
        target[...] = jnp.dot(
            hidden, w_ref[0, m], preferred_element_type=jnp.float32
        ).astype(jnp.bfloat16)
    jobs = [
        (h, c, c * pairs + k)
        for h in range(part // HD)
        for c in range(blocks)
        for k in range(pairs)
    ]

    def span_of(h, unit):
        return slice(unit * length, (unit + 1) * length), slice(h * HD, (h + 1) * HD)

    scores = []
    for h, c, unit in jobs:
        span, columns = span_of(h, unit)
        query = q_s[span, columns]
        near = lax.dot_general(query, k_s[span, columns], NT, preferred_element_type=jnp.float32)
        far = lax.dot_general(
            query, cond_ref[0, 0, c, :, columns], NT, preferred_element_type=jnp.float32
        )
        bias = bias_ref[step * (part // HD) + h]
        scores.append((near * SCALE + bias * hit_ref[unit], far * SCALE))
    tops = [
        jnp.maximum(
            jnp.max(near, axis=-1, keepdims=True), jnp.max(far, axis=-1, keepdims=True)
        )
        for near, far in scores
    ]
    scores = [(jnp.exp(near - top), jnp.exp(far - top)) for (near, far), top in zip(scores, tops)]
    shares = [
        1.0 / (jnp.sum(near, axis=-1, keepdims=True) + jnp.sum(far, axis=-1, keepdims=True))
        for near, far in scores
    ]
    results = []
    for (h, c, unit), (near, far), share in zip(jobs, scores, shares):
        span, columns = span_of(h, unit)
        results.append(
            jnp.dot(
                (near * share).astype(jnp.bfloat16),
                v_s[span, columns],
                preferred_element_type=jnp.float32,
            )
            + jnp.dot(
                (far * share).astype(jnp.bfloat16),
                cond_ref[0, 1, c, :, columns],
                preferred_element_type=jnp.float32,
            )
        )
    for (h, c, unit), result in zip(jobs, results):
        span, columns = span_of(h, unit)
        mixed[span, columns] = result.astype(jnp.bfloat16)
    total[...] += lax.dot_general(
        mixed[...], w_ref[0, 3], NT, preferred_element_type=jnp.float32
    )

    @pl.when(step == tp_size - 1)
    def _():
        encoded = total[...].astype(jnp.bfloat16)
        for p in range(tp_size):
            kv_ref[p] = jnp.dot(
                encoded, cca_ref[p, 0], preferred_element_type=jnp.float32
            ).astype(jnp.bfloat16)


def softmax_rows(scores):
    scores = jnp.exp(scores - jnp.max(scores, axis=-1, keepdims=True))
    return (scores * (1.0 / jnp.sum(scores, axis=-1, keepdims=True))).astype(jnp.bfloat16)


def attend_kernel(allowed_ref, q_ref, prev_ref, cur_ref, out_ref):
    block = pl.program_id(0)
    tokens = q_ref.shape[0]
    heads = q_ref.shape[1] // HD
    query = q_ref[...]
    stacked = jnp.concatenate([query[:, h * HD : (h + 1) * HD] for h in range(heads)], axis=0)
    ok = allowed_ref[block] > 0

    def mix(rows, kv_ref):
        scores = lax.dot_general(
            rows, kv_ref[:, :HD], NT, preferred_element_type=jnp.float32
        ) * SCALE
        return jnp.dot(
            softmax_rows(scores), kv_ref[:, HD:], preferred_element_type=jnp.float32
        )

    leading = mix(stacked, prev_ref)
    tail = query[tokens - 16 :, :]
    tails = jnp.concatenate([tail[:, h * HD : (h + 1) * HD] for h in range(heads)], axis=0)
    trailing = mix(tails, cur_ref)
    last = lax.broadcasted_iota(jnp.int32, (16, HD), 0) == 15
    for h in range(heads):
        columns = slice(h * HD, (h + 1) * HD)
        value = leading[h * tokens : (h + 1) * tokens]
        value = jnp.where(ok, value, jnp.zeros_like(value))
        out_ref[: tokens - 16, columns] = value[: tokens - 16].astype(jnp.bfloat16)
        out_ref[tokens - 16 :, columns] = jnp.where(
            last, trailing[h * 16 : (h + 1) * 16], value[tokens - 16 :]
        ).astype(jnp.bfloat16)


def shards(
    db_tokens,
    db_parent,
    db_depth,
    nb_rows,
    seq_start,
    table,
    depth_table,
    enc_gain,
    enc_qkv,
    tree_bias,
    enc_wo,
    cond_kv,
    queries,
    cca_kv,
):
    seq_size = lax.axis_size("seq")
    tp_size = lax.axis_size("tp")
    block_count, pair_count = nb_rows.shape
    unit_count = block_count * pair_count
    stored, length = db_tokens.shape
    slot_count = max(1, 2 * unit_count // seq_size)
    part = enc_qkv.shape[2]
    rows = enc_qkv.shape[0]
    width = part * tp_size
    cond_len = cond_kv.shape[0] // block_count
    bf16 = jnp.bfloat16
    anywhere = pl.BlockSpec(memory_space=pl.ANY)
    vmem = pl.BlockSpec(memory_space=pltpu.VMEM)
    dma = pltpu.SemaphoreType.DMA

    flat_rows = nb_rows.reshape(unit_count)
    holder = flat_rows // stored
    local_row = flat_rows % stored
    ordering = jnp.arange(unit_count, dtype=jnp.int32)
    earlier = jnp.sum(
        ((holder[:, None] == holder[None, :]) & (ordering[:, None] > ordering[None, :])).astype(
            jnp.int32
        ),
        axis=1,
    )
    target = holder * 8 + earlier
    places = jnp.arange(seq_size * 8, dtype=jnp.int32)
    request = jnp.sum(
        jnp.where(target[None, :] == places[:, None], local_row[None, :], 0), axis=1
    )
    request = jnp.broadcast_to(request.reshape(seq_size, 8, 1), (seq_size, 8, 128))
    packed = jnp.concatenate(
        [
            enc_qkv.transpose(1, 0, 2),
            enc_wo.T[None],
            cca_kv.reshape(1, rows, part),
        ],
        axis=0,
    )
    cond = cond_kv.transpose(1, 0, 2)
    share = unit_count // tp_size
    block_share = block_count // tp_size
    response, own_cond = pl.pallas_call(
        functools.partial(fetch_kernel, seq_size, tp_size),
        out_shape=(
            jax.ShapeDtypeStruct((seq_size, 8, 384), jnp.int32),
            jax.ShapeDtypeStruct((tp_size, 2, block_share * cond_len, part), bf16),
        ),
        in_specs=[vmem] + [anywhere] * 4,
        out_specs=(vmem, anywhere),
        scratch_shapes=[
            pltpu.VMEM((seq_size, 8, 128), jnp.int32),
            pltpu.VMEM((seq_size, 8, 384), jnp.int32),
            pltpu.VMEM((stored, length), jnp.int32),
            pltpu.VMEM((stored, length), jnp.int32),
            pltpu.VMEM((stored, length), jnp.int32),
            dma((3,)),
            dma,
            dma((seq_size,)),
            dma((seq_size,)),
            dma((seq_size,)),
            dma((seq_size,)),
            dma((tp_size,)),
            dma((tp_size,)),
        ],
        compiler_params=pltpu.CompilerParams(
            collective_id=0, has_side_effects=True, vmem_limit_bytes=12 << 20
        ),
        name="fetch_rows",
    )(request, db_tokens, db_depth, db_parent, cond)

    answer = jnp.take(response.reshape(seq_size * 8, 384), target, axis=0, mode="clip")
    tokens = answer[:, :length].reshape(unit_count * length)
    depths = answer[:, length : 2 * length].reshape(unit_count * length)
    parents = lax.dynamic_slice_in_dim(
        answer[:, 2 * length :], lax.axis_index("tp") * share, share, 0
    )
    hit = (parents[:, :, None] == jnp.arange(length, dtype=jnp.int32)).astype(jnp.float32)
    depth_pick = (
        depths[:, None] == jnp.arange(depth_table.shape[0], dtype=jnp.int32)[None, :]
    ).astype(bf16)
    embedded = (
        jnp.take(table, tokens, axis=0, mode="clip").astype(jnp.float32)
        + jnp.dot(depth_pick, depth_table, preferred_element_type=jnp.float32)
    ).astype(bf16)

    mine = share * length
    full, own_emb = pl.pallas_call(
        functools.partial(gather_kernel, seq_size, tp_size),
        out_shape=(
            jax.ShapeDtypeStruct((tp_size, 5, width, part), bf16),
            jax.ShapeDtypeStruct((tp_size, mine, part), bf16),
        ),
        in_specs=[anywhere] * 2,
        out_specs=(anywhere, anywhere),
        scratch_shapes=[
            dma((2, seq_size * tp_size)),
            dma((2, seq_size * tp_size)),
            dma((3,)),
            dma((tp_size,)),
            dma((tp_size,)),
        ],
        compiler_params=pltpu.CompilerParams(collective_id=1, has_side_effects=True),
        name="gather_weights_and_embedded",
    )(packed, embedded)

    cond_blocks = own_cond.reshape(tp_size, 2, block_share, cond_len, part)
    keys_values = pl.pallas_call(
        functools.partial(encoder_kernel, tp_size, length, pair_count),
        grid=(tp_size,),
        out_shape=jax.ShapeDtypeStruct((tp_size, mine, part), bf16),
        in_specs=[
            pl.BlockSpec(memory_space=pltpu.SMEM),
            pl.BlockSpec((tp_size, mine, part), lambda i: (0, 0, 0)),
            pl.BlockSpec((1, width), lambda i: (0, 0)),
            pl.BlockSpec((1, 4, width, part), lambda i: (i, 0, 0, 0)),
            pl.BlockSpec((tp_size, 1, width, part), lambda i: (0, 4, 0, 0)),
            pl.BlockSpec((1, 2, block_share, cond_len, part), lambda i: (i, 0, 0, 0, 0)),
            pl.BlockSpec((share, length, length), lambda i: (0, 0, 0)),
        ],
        out_specs=pl.BlockSpec((tp_size, mine, part), lambda i: (0, 0, 0)),
        scratch_shapes=[
            pltpu.VMEM((mine, width), bf16),
            pltpu.VMEM((mine, width), jnp.float32),
            pltpu.VMEM((mine, part), bf16),
            pltpu.VMEM((mine, part), bf16),
            pltpu.VMEM((mine, part), bf16),
            pltpu.VMEM((mine, part), bf16),
        ],
        compiler_params=pltpu.CompilerParams(vmem_limit_bytes=56 << 20),
        name="encode",
    )(tree_bias, own_emb, enc_gain.reshape(1, width), full, full, cond_blocks, hit)

    key_rows = pair_count * length
    spread = pl.pallas_call(
        functools.partial(spread_kernel, seq_size, tp_size),
        out_shape=jax.ShapeDtypeStruct(((block_count + 1) * key_rows, part), bf16),
        in_specs=[anywhere],
        out_specs=anywhere,
        scratch_shapes=[dma((tp_size,)), dma((tp_size,)), dma((tp_size,)), dma, dma],
        compiler_params=pltpu.CompilerParams(collective_id=2, has_side_effects=True, vmem_limit_bytes=56 << 20),
        name="spread_keys_values",
    )(keys_values)

    block_index = lax.axis_index("seq") * block_count + jnp.arange(block_count, dtype=jnp.int32)
    allowed = ((block_index > 0) & (seq_start == 0)).astype(jnp.int32)
    columns = queries.shape[1]
    return pl.pallas_call(
        attend_kernel,
        grid=(block_count,),
        out_shape=jax.ShapeDtypeStruct(queries.shape, bf16),
        in_specs=[
            pl.BlockSpec(memory_space=pltpu.SMEM),
            pl.BlockSpec((cond_len, columns), lambda i: (i, 0)),
            pl.BlockSpec((key_rows, part), lambda i: (i, 0)),
            pl.BlockSpec((key_rows, part), lambda i: (i + 1, 0)),
        ],
        out_specs=pl.BlockSpec((cond_len, columns), lambda i: (i, 0)),
        compiler_params=pltpu.CompilerParams(vmem_limit_bytes=56 << 20),
        name="attend",
    )(allowed, queries, spread, spread)


def solution(mesh):
    in_specs = (
        P("seq", None),
        P("seq", None),
        P("seq", None),
        P("seq", None),
        P("seq"),
        P(None, "tp"),
        P(None, "tp"),
        P(),
        P("seq", None, "tp"),
        P(),
        P("tp", "seq"),
        P("seq", None, "tp"),
        P("seq", "tp"),
        P("seq", None, "tp"),
    )
    out_specs = P("seq", "tp")
    return jax.shard_map(shards, mesh=mesh, in_specs=in_specs, out_specs=out_specs, check_vma=False)
```
